32 devices in a mesh: grp: 4 (over y, x), rep: 4 (over z), tp: 2 (over core).
Axes of the slice: x: 2, y: 2, z: 4, core: 2. Of those that a mesh axis runs over, the one named last changes fastest.
Arguments:
- noise_in: bfloat16 [512, 3072], P('rep', 'tp'), may hold values from -6 to 6
- noise_renoise: bfloat16 [512, 3072], P('rep', 'tp'), may hold values from -6 to 6
- text_cond: bfloat16 [4, 3072], P('rep'), may hold values from -3 to 3
- t_index: int32 [4], P('rep'), may hold values from 0 to 999
- gains: float32 [3, 3072], replicated, may hold values from 0.5 to 1.5
- up_weights: bfloat16 [3, 3072, 12288], P(None, 'rep', 'tp'), may hold values from -0.109375 to 0.109375
- down_weights: bfloat16 [3, 12288, 3072], P(None, 'tp', 'rep'), may hold values from -0.0546875 to 0.0546875
Outputs:
- generated: bfloat16 [512, 3072], P('rep', 'tp')
- up_grads: float32 [4, 3072, 12288], P('grp', 'rep', 'tp')
- down_grads: float32 [4, 12288, 3072], P('grp', 'tp', 'rep')
The draws below stay inside these ranges and needn't reach their ends.
All inputs are finite; a program needn't handle non-finite values. Where the reference program divides by a largest or mean magnitude, that divisor is 1e-20 or more.
Results may differ from the reference program's by a relative error of at most 0.01.
Values may be sent and summed in bfloat16 or wider, within the bound.
No kernel may reach another device: no remote copies, remote signals or barrier semaphores. Data moves between devices by JAX's collectives and lax.ppermute only.
A program may use at most 256 MiB of HBM per device.

```python
import jax
import jax.numpy as jnp
from jax import lax

D = 3072
HID = 12288
IMG_TOK = 128
TOK_DEV = 128
TOKENS = 512
IMAGES = 4


def touch_ends(drawn, own_key, low, high):
    extent = drawn.shape
    spot = [jax.random.randint(jax.random.fold_in(own_key, axis), (), 0, extent[axis]) for axis in range(len(extent))]
    drawn = drawn.at[tuple(spot)].set(low)
    longest = extent.index(max(extent))
    spot[longest] = (spot[longest] + 1) % extent[longest]
    return drawn.at[tuple(spot)].set(high)


def block_scale(stream_key, dims, split, least, largest):
    def one(axis_at, blocks):
        draws = jax.random.uniform(jax.random.fold_in(jax.random.fold_in(stream_key, 6), axis_at), (blocks,), jnp.float32, least / len(split), largest / len(split))
        return jnp.repeat(jnp.exp(draws), dims[axis_at] // blocks).reshape((-1,) + (1,) * (len(dims) - axis_at - 1))

    factor_of = one(*split[0])
    for cut in split[1:]:
        factor_of = factor_of * one(*cut)
    return factor_of


def bell_draw(own_key, dims, scale, most, cuts=(), kind=jnp.bfloat16):
    result = scale * jax.random.normal(own_key, dims, jnp.float32)
    if cuts:
        result = result * block_scale(own_key, dims, cuts, -0.22, 0.18)
    return jnp.clip(result, -most, most).astype(kind)


def setup_inputs(seed: int = 0) -> dict:
    seeds = jax.random.split(jax.random.key(seed), 8)
    return {
        "noise_in": bell_draw(seeds[0], (TOKENS, D), 1.0, 6.0, ((0, 4), (1, 2))),
        "noise_renoise": bell_draw(seeds[1], (TOKENS, D), 1.0, 6.0, ((0, 4), (1, 2))),
        "text_cond": bell_draw(seeds[2], (IMAGES, D), 0.5, 3.0, ((0, 4),)),
        "t_index": touch_ends(jax.random.randint(seeds[3], (IMAGES,), 0, 1000), jax.random.fold_in(seeds[3], 1), 0, 999).astype(jnp.int32),
        "gains": jnp.clip(1.0 + 0.1 * jax.random.normal(seeds[4], (3, D), jnp.float32), 0.5, 1.5),
        "up_weights": bell_draw(seeds[5], (3, D, HID), D ** -0.5, 0.109375, ((1, 4), (2, 2))),
        "down_weights": bell_draw(seeds[6], (3, HID, D), HID ** -0.5, 0.0546875, ((1, 2), (2, 4))),
    }


def gelu_tanh(value):
    return jax.nn.gelu(value, approximate=True)

def front_pass(inputs, gain_row, cond_rows, up_matrix):
    values = inputs.astype(jnp.float32)
    factor = lax.rsqrt(lax.optimization_barrier(jnp.mean(values * values, axis=-1, keepdims=True)) + 1e-06)
    normed = (values * factor * gain_row[None, :] * (1.0 + cond_rows)).astype(jnp.bfloat16)
    hidden_pre = jnp.dot(normed, up_matrix, preferred_element_type=jnp.float32)
    hidden = gelu_tanh(hidden_pre).astype(jnp.bfloat16)
    return (normed, hidden_pre, hidden)

def block_pass(inputs, gain_row, cond_rows, up_matrix, down_matrix):
    normed, hidden_pre, hidden = front_pass(inputs, gain_row, cond_rows, up_matrix)
    output = (inputs.astype(jnp.float32) + jnp.dot(hidden, down_matrix, preferred_element_type=jnp.float32)).astype(jnp.bfloat16)
    return (output, normed, hidden_pre, hidden)

def backward(normed, hidden_pre, hidden, upstream, down_matrix):
    down_grad = jnp.dot(hidden.T, upstream, preferred_element_type=jnp.float32)
    hidden_grad = jnp.dot(upstream, down_matrix.T, preferred_element_type=jnp.float32)
    pre_grad = jax.vjp(gelu_tanh, hidden_pre)[1](hidden_grad)[0].astype(jnp.bfloat16)
    up_grad = jnp.dot(normed.T, pre_grad, preferred_element_type=jnp.float32)
    return (up_grad, down_grad)

def reference(noise_in, noise_renoise, text_cond, t_index, gains, up_weights, down_weights):
    cond_rows = jnp.repeat(text_cond.astype(jnp.float32), IMG_TOK, axis=0)
    generated, normed_s, pre_s, hidden_s = block_pass(noise_in, gains[0], cond_rows, up_weights[0], down_weights[0])
    sigma = 0.1 + 0.8 * t_index.astype(jnp.float32) / 999.0
    sigma_rows = jnp.repeat(sigma, IMG_TOK)[:, None]
    noised = ((1.0 - sigma_rows) * generated.astype(jnp.float32) + sigma_rows * noise_renoise.astype(jnp.float32)).astype(jnp.bfloat16)
    real_out = block_pass(noised, gains[1], cond_rows, up_weights[1], down_weights[1])[0]
    fake_out, normed_f, pre_f, hidden_f = block_pass(noised, gains[2], cond_rows, up_weights[2], down_weights[2])
    gen_f = generated.astype(jnp.float32)
    real_f = real_out.astype(jnp.float32)
    fake_f = fake_out.astype(jnp.float32)
    images = t_index.shape[0]
    image_norm = lax.optimization_barrier(jnp.mean(jnp.abs(gen_f - real_f).reshape(images, -1), axis=1)) + 1e-05
    push_scale = 1.0 / jnp.sqrt(jnp.float32(TOKENS))
    student_push = ((fake_f - real_f) / jnp.repeat(image_norm, IMG_TOK)[:, None] * push_scale).astype(jnp.bfloat16)
    fake_push = ((fake_f - gen_f) * push_scale).astype(jnp.bfloat16)
    position = jnp.arange(TOKENS, dtype=jnp.int32) % TOK_DEV
    first_half = (position < TOK_DEV // 2)[:, None]
    zeros_push = jnp.zeros_like(student_push)
    push_first = jnp.where(first_half, student_push, zeros_push)
    push_second = jnp.where(first_half, zeros_push, student_push)
    up_a, down_a = backward(normed_s, pre_s, hidden_s, push_first, down_weights[0])
    up_b, down_b = backward(normed_s, pre_s, hidden_s, push_second, down_weights[0])
    up_f, down_f = backward(normed_f, pre_f, hidden_f, fake_push, down_weights[2])
    up_grads = jnp.stack([up_a, up_b, jnp.zeros_like(up_f), up_f])
    down_grads = jnp.stack([down_a, down_b, jnp.zeros_like(down_f), down_f])
    return (generated, up_grads, down_grads)
```

```python
import math

import jax
import jax.numpy as jnp
from jax import lax
from jax.sharding import PartitionSpec as P

IMG_TOK = 128
CHUNKS = 2
LOCKSTEP = True
F32 = jnp.float32
BF16 = jnp.bfloat16

INWARD = ((0, 1), (3, 2))
ACROSS = ((1, 2), (2, 1))
OUTWARD = ((1, 0), (2, 3))


def gelu_tanh(value):
    return jax.nn.gelu(value, approximate=True)


def dot(left, right):
    return jnp.dot(left, right, preferred_element_type=F32)


def dot_transposed(left, right):
    return lax.dot_general(left, right, (((1,), (1,)), ((), ())), preferred_element_type=F32)


def together(*tasks):
    tasks = list(tasks)
    results = [None] * len(tasks)
    inbox = [None] * len(tasks)
    active = list(range(len(tasks)))
    while active:
        sends, owners, still = [], [], []
        for i in active:
            try:
                messages = tasks[i].send(inbox[i])
            except StopIteration as stop:
                results[i] = stop.value
                continue
            owners.append((i, len(messages)))
            sends += messages
            still.append(i)
        active = still
        if not active:
            break
        received = yield sends
        at = 0
        for i, count in owners:
            inbox[i] = received[at : at + count]
            at += count
    return results


def delayed(rounds, task):
    for _ in range(rounds):
        yield []
    return (yield from task)


def drive(task):
    inbox, last = None, []
    while True:
        try:
            sends = task.send(inbox)
        except StopIteration as stop:
            return stop.value
        payloads = [payload for _, payload in sends]
        if LOCKSTEP and last and payloads:
            payloads, _ = lax.optimization_barrier((payloads, last))
        inbox = [lax.ppermute(v, "rep", pairs) for (pairs, _), v in zip(sends, payloads)]
        if inbox:
            last = inbox


def butterfly(value, axis):
    size = lax.axis_size(axis)
    step = 1
    while step < size:
        value = value + lax.ppermute(value, axis, [(i, i ^ step) for i in range(size)])
        step *= 2
    return value


def tp_sum(value):
    size = lax.axis_size("tp")
    if size == 2:
        return value + lax.ppermute(value, "tp", [(0, 1), (1, 0)])
    return lax.psum(value, "tp")


def reduce_line(partial):
    size = lax.axis_size("rep")
    if size != 4:
        return lax.psum(partial, "rep")
    lower = lax.axis_index("rep") < 2
    half = partial.shape[1] // 2
    low, high = partial[:, :half], partial[:, half:]
    first = jnp.where(lower, high, low)
    second = jnp.where(lower, low, high)
    (got,) = yield [(INWARD, first.astype(BF16))]
    (got,) = yield [(ACROSS, (first + got.astype(F32)).astype(BF16))]
    second = second + got.astype(F32)
    (got,) = yield [(OUTWARD, second.astype(BF16))]
    return second + got.astype(F32)


def spread_line(own):
    size = lax.axis_size("rep")
    if size != 4:
        return own
    index = lax.axis_index("rep")
    lower = index < 2
    end = (index == 0) | (index == 3)
    (got,) = yield [(INWARD, own)]
    second = jnp.where(end, own, got)
    (first_mid,) = yield [(ACROSS, second)]
    (first_end,) = yield [(OUTWARD, first_mid)]
    first = jnp.where(end, first_end, first_mid)
    return jnp.concatenate([jnp.where(lower, second, first), jnp.where(lower, first, second)], axis=1)


def forward(normed, factor, up, down):
    pre = yield from reduce_line(dot(normed, up))
    if factor is not None:
        pre = pre * factor
    hidden = yield from spread_line(gelu_tanh(pre).astype(BF16))
    return pre, hidden, tp_sum(dot(hidden, down))


def backward(upstream, scale, pre, down):
    grad = yield from reduce_line(dot_transposed(upstream, down))
    if scale is not None:
        grad = grad * scale
    pre_grad = jax.vjp(gelu_tanh, pre)[1](grad)[0].astype(BF16)
    return (yield from spread_line(pre_grad))


def body(noise_in, noise_renoise, text_cond, t_index, gains, up_weights, down_weights):
    g, r = lax.axis_index("grp"), lax.axis_index("rep")
    groups, reps = lax.axis_size("grp"), lax.axis_size("rep")
    rows = noise_in.shape[0]
    images = t_index.shape[0]
    n = rows // groups
    width = gains.shape[1]
    own_width = width // reps
    quarter = (g % 2) * (groups // 2) + g // 2
    image_of = (quarter * n + jnp.arange(n)) // IMG_TOK

    def mine(whole):
        return lax.dynamic_slice_in_dim(whole, quarter * n, n, 0)

    both = jnp.concatenate([mine(noise_in), mine(noise_renoise)], axis=0)
    both = lax.all_gather(both, "tp", axis=1, tiled=True)
    values = both[:n].astype(F32)
    cond = text_cond.astype(F32)
    cond_rows = jnp.broadcast_to(cond, (n, width)) if images == 1 else jnp.take(cond, image_of, axis=0)
    factor = lax.rsqrt(jnp.mean(values * values, axis=-1, keepdims=True) + 1e-06)
    normed = (values * factor * gains[0][None, :] * (1.0 + cond_rows)).astype(BF16)
    normed = lax.all_to_all(normed, "rep", split_axis=1, concat_axis=0, tiled=True)

    high = (t_index // 256).astype(BF16)
    low = (t_index % 256).astype(BF16)
    extra = 3 * images
    pad = -(2 * n + extra) % 16
    side = jnp.concatenate(
        [
            both,
            text_cond,
            jnp.broadcast_to(high[:, None], (images, width)),
            jnp.broadcast_to(low[:, None], (images, width)),
            jnp.zeros((pad, width), BF16),
        ],
        axis=0,
    )
    side = lax.all_to_all(side, "rep", split_axis=1, concat_axis=0, tiled=True)
    side = side.reshape(reps, 2 * n + extra + pad, own_width)

    def per_row(block):
        if images == 1:
            spread = jnp.broadcast_to(block, (reps, n, block.shape[-1]))
        else:
            spread = jnp.take(block, image_of, axis=1)
        return spread.reshape(reps * n, block.shape[-1])

    at = 2 * n
    x_in = side[:, :n].reshape(reps * n, own_width)
    renoise = side[:, n:at].reshape(reps * n, own_width)
    cond_part = 1.0 + per_row(side[:, at : at + images].astype(F32))
    steps = side[:, at + images : at + 3 * images, :1].astype(F32)
    t_values = steps[:, :images] * 256.0 + steps[:, images:]
    sigma = per_row(0.1 + 0.8 * t_values / 999.0)
    own_gains = lax.dynamic_slice_in_dim(gains, r * own_width, own_width, 1)

    total = reps * n
    push_scale = 1.0 / math.sqrt(rows * reps)
    image_rows = jnp.repeat(jnp.arange(reps), n) * images + jnp.tile(image_of, reps)

    def image_sums(part):
        count = part.shape[0] // n
        if images == 1:
            sums = butterfly(butterfly(jnp.sum(part.reshape(count, n), axis=1), "rep"), "grp")
            return jnp.repeat(sums, n)[:, None]
        hot = (image_rows[:, None] == jnp.arange(reps * images)[None, :]).astype(F32)
        hot = hot[: part.shape[0]]
        sums = butterfly(butterfly(jnp.sum(part[:, None] * hot, axis=0), "rep"), "grp")
        return jnp.sum(hot * sums[None, :], axis=1, keepdims=True)

    def chain(at, count):
        def cut(whole):
            return whole[at : at + count]

        x, cond_1, sig = cut(x_in).astype(F32), cut(cond_part), cut(sigma)
        pre_s, hidden_s, out = yield from forward(cut(normed), None, up_weights[0], down_weights[0])
        made = (x + out).astype(BF16)
        made_f = made.astype(F32)
        noised = ((1.0 - sig) * made_f + sig * cut(renoise).astype(F32)).astype(BF16)
        noised_f = noised.astype(F32)
        squares = butterfly(jnp.sum(noised_f * noised_f, axis=1), "rep")[:, None]
        factor = lax.rsqrt(squares / width + 1e-06)
        scaled = noised_f * cond_1
        teacher = forward((scaled * own_gains[1][None, :]).astype(BF16), factor, up_weights[1], down_weights[1])
        fake = forward((scaled * own_gains[2][None, :]).astype(BF16), factor, up_weights[2], down_weights[2])
        (_, _, out_t), (pre_f, hidden_f, out_f) = yield from together(teacher, delayed(1, fake))
        real_f = (noised_f + out_t).astype(BF16).astype(F32)
        fake_f = (noised_f + out_f).astype(BF16).astype(F32)
        push_f = ((fake_f - made_f) * push_scale).astype(BF16)
        raw_s = (fake_f - real_f) * push_scale
        distance = image_sums(jnp.sum(jnp.abs(made_f - real_f), axis=1))
        inverse = 1.0 / (distance / (IMG_TOK * width) + 1e-05)
        grad_f, grad_s = yield from together(
            backward(push_f, None, pre_f, down_weights[2]),
            delayed(1, backward(raw_s.astype(BF16), inverse, pre_s, down_weights[0])),
        )
        push_s = (raw_s * inverse).astype(BF16)
        normed_f = (noised_f * factor * own_gains[2][None, :] * cond_1).astype(BF16)
        return made, (cut(normed), push_s, hidden_s, grad_s), (normed_f, push_f, hidden_f, grad_f)

    chunks = CHUNKS if images == 1 and reps % CHUNKS == 0 else 1
    count = total // chunks
    parts = drive(together(*[delayed(2 * c, chain(c * count, count)) for c in range(chunks)]))

    made = jnp.concatenate([p[0] for p in parts], axis=0)
    made = lax.all_to_all(made, "rep", split_axis=0, concat_axis=1, tiled=True)
    tp_width = noise_in.shape[1]
    made = lax.dynamic_slice_in_dim(made, lax.axis_index("tp") * tp_width, tp_width, 1)
    made = lax.all_gather(made, "grp", axis=0)
    generated = jnp.concatenate([made[i] for i in (0, 2, 1, 3)], axis=0)

    is_fake = g == 3
    keep = g != 2

    def gather_rows(student, fake, masked):
        own = jnp.where(is_fake, fake, student)
        if masked:
            own = jnp.where(keep, own, jnp.zeros_like(own))
        from_y = jnp.where(
            is_fake,
            lax.ppermute(fake, "grp", ((1, 3),)),
            lax.ppermute(student, "grp", ((2, 0), (3, 1))),
        )
        from_x = lax.ppermute(fake, "grp", ((2, 3),))
        from_d = lax.ppermute(fake, "grp", ((0, 3),))
        return [own, from_y, from_x, from_d]

    gathered = []
    for k in range(4):
        blocks = []
        for _, student, fake in parts:
            blocks += gather_rows(student[k], fake[k], k < 2)
        gathered.append(jnp.concatenate(blocks, axis=0))
    normed_all, push_all, hidden_all, grad_all = gathered
    down_grad = dot(hidden_all.T, push_all)
    up_grad = dot(normed_all.T, grad_all)
    return (generated, up_grad[None], down_grad[None])


def solution(mesh):
    in_specs = (
        P("rep", "tp"),
        P("rep", "tp"),
        P("rep", None),
        P("rep"),
        P(),
        P(None, "rep", "tp"),
        P(None, "tp", "rep"),
    )
    out_specs = (P("rep", "tp"), P("grp", "rep", "tp"), P("grp", "tp", "rep"))
    return jax.shard_map(body, mesh=mesh, in_specs=in_specs, out_specs=out_specs, check_vma=False)
```

```python
import math

import jax
import jax.numpy as jnp
from jax import lax
from jax.sharding import PartitionSpec as P

IMG_TOK = 128
FIRST_PARTS, PARTS, TEACHER_AT, MADE_AT, PAIR_AT = 2, 2, 2, 0, 5
F32 = jnp.float32
BF16 = jnp.bfloat16

INWARD = ((0, 1), (3, 2))
ACROSS = ((1, 2), (2, 1))
OUTWARD = ((1, 0), (2, 3))


def gelu_tanh(value):
    return jax.nn.gelu(value, approximate=True)


def dot(left, right):
    return jnp.dot(left, right, preferred_element_type=F32)


def dot_transposed(left, right):
    return lax.dot_general(left, right, (((1,), (1,)), ((), ())), preferred_element_type=F32)


def together(*tasks):
    tasks = list(tasks)
    results = [None] * len(tasks)
    inbox = [None] * len(tasks)
    active = list(range(len(tasks)))
    while active:
        sends, owners, still = [], [], []
        for i in active:
            try:
                messages = tasks[i].send(inbox[i])
            except StopIteration as stop:
                results[i] = stop.value
                continue
            owners.append((i, len(messages)))
            sends += messages
            still.append(i)
        active = still
        if not active:
            break
        received = yield sends
        at = 0
        for i, count in owners:
            inbox[i] = received[at : at + count]
            at += count
    return results


def delayed(rounds, task):
    for _ in range(rounds):
        yield []
    return (yield from task)


def staggered(tasks):
    return together(*[delayed(i, task) for i, task in enumerate(tasks)])


class Order:
    def __init__(self):
        self.before = None

    def after(self, value):
        if self.before is not None:
            value, _ = lax.optimization_barrier((value, self.before))
        return value

    def drive(self, task):
        inbox = None
        while True:
            try:
                sends = task.send(inbox)
            except StopIteration as stop:
                return stop.value
            inbox = []
            for axis, pairs, payload in sends:
                self.before = self.after(payload)
                inbox.append(lax.ppermute(self.before, axis, pairs))


def butterfly(value, axis):
    size = lax.axis_size(axis)
    step = 1
    while step < size:
        (got,) = yield [(axis, [(i, i ^ step) for i in range(size)], value)]
        value = value + got
        step *= 2
    return value


def tp_sum(value):
    size = lax.axis_size("tp")
    if size == 2:
        return value + lax.ppermute(value, "tp", [(0, 1), (1, 0)])
    return lax.psum(value, "tp")


def reduce_line(partial):
    size = lax.axis_size("rep")
    if size != 4:
        return lax.psum(partial, "rep")
    lower = lax.axis_index("rep") < 2
    half = partial.shape[1] // 2
    low, high = partial[:, :half], partial[:, half:]
    first = jnp.where(lower, high, low)
    second = jnp.where(lower, low, high)
    (got,) = yield [("rep", INWARD, first.astype(BF16))]
    (got,) = yield [("rep", ACROSS, (first + got.astype(F32)).astype(BF16))]
    second = second + got.astype(F32)
    (got,) = yield [("rep", OUTWARD, second.astype(BF16))]
    return second + got.astype(F32)


def spread_line(own):
    size = lax.axis_size("rep")
    if size != 4:
        return own
    index = lax.axis_index("rep")
    lower = index < 2
    end = (index == 0) | (index == 3)
    (got,) = yield [("rep", INWARD, own)]
    second = jnp.where(end, own, got)
    (first_mid,) = yield [("rep", ACROSS, second)]
    (first_end,) = yield [("rep", OUTWARD, first_mid)]
    first = jnp.where(end, first_end, first_mid)
    return jnp.concatenate([jnp.where(lower, second, first), jnp.where(lower, first, second)], axis=1)


def forward(order, normed, factor, up, down):
    pre = yield from reduce_line(dot(order.after(normed), up))
    if factor is not None:
        pre = pre * (yield from factor())
    hidden = yield from spread_line(gelu_tanh(pre).astype(BF16))
    return pre, hidden, dot(hidden, down)


def backward(order, upstream, pre, down):
    grad = yield from reduce_line(dot_transposed(order.after(upstream), down))
    pre_grad = jax.vjp(gelu_tanh, pre)[1](grad)[0].astype(BF16)
    return (yield from spread_line(pre_grad))


def body(noise_in, noise_renoise, text_cond, t_index, gains, up_weights, down_weights):
    g, r = lax.axis_index("grp"), lax.axis_index("rep")
    groups, reps = lax.axis_size("grp"), lax.axis_size("rep")
    rows = noise_in.shape[0]
    images = t_index.shape[0]
    n = rows // groups
    width = gains.shape[1]
    own_width = width // reps
    quarter = (g % 2) * (groups // 2) + g // 2
    image_of = (quarter * n + jnp.arange(n)) // IMG_TOK

    def mine(whole):
        return lax.dynamic_slice_in_dim(whole, quarter * n, n, 0)

    both = jnp.concatenate([mine(noise_in), mine(noise_renoise)], axis=0)
    both = lax.all_gather(both, "tp", axis=1, tiled=True)
    values = both[:n].astype(F32)
    cond = text_cond.astype(F32)
    cond_rows = jnp.broadcast_to(cond, (n, width)) if images == 1 else jnp.take(cond, image_of, axis=0)
    factor = lax.rsqrt(jnp.mean(values * values, axis=-1, keepdims=True) + 1e-06)
    normed = (values * factor * gains[0][None, :] * (1.0 + cond_rows)).astype(BF16)
    normed = lax.all_to_all(normed, "rep", split_axis=1, concat_axis=0, tiled=True)

    high = (t_index // 256).astype(BF16)
    low = (t_index % 256).astype(BF16)
    extra = 3 * images
    pad = -(2 * n + extra) % 16
    side = jnp.concatenate(
        [
            both,
            text_cond,
            jnp.broadcast_to(high[:, None], (images, width)),
            jnp.broadcast_to(low[:, None], (images, width)),
            jnp.zeros((pad, width), BF16),
        ],
        axis=0,
    )
    side = lax.all_to_all(side, "rep", split_axis=1, concat_axis=0, tiled=True)
    side = side.reshape(reps, 2 * n + extra + pad, own_width)

    def per_row(block):
        if images == 1:
            spread = jnp.broadcast_to(block, (reps, n, block.shape[-1]))
        else:
            spread = jnp.take(block, image_of, axis=1)
        return spread.reshape(reps * n, block.shape[-1])

    at = 2 * n
    x_in = side[:, :n].reshape(reps * n, own_width)
    renoise = side[:, n:at].reshape(reps * n, own_width)
    cond_part = 1.0 + per_row(side[:, at : at + images].astype(F32))
    steps = side[:, at + images : at + 3 * images, :1].astype(F32)
    t_values = steps[:, :images] * 256.0 + steps[:, images:]
    sigma = per_row(0.1 + 0.8 * t_values / 999.0)
    own_gains = lax.dynamic_slice_in_dim(gains, r * own_width, own_width, 1)

    push_scale = 1.0 / math.sqrt(rows * reps)
    image_rows = jnp.repeat(jnp.arange(reps), n) * images + jnp.tile(image_of, reps)

    def image_sums(part):
        if images == 1:
            sums = jnp.sum(part.reshape(reps, n), axis=1)
        else:
            hot = (image_rows[:, None] == jnp.arange(reps * images)[None, :]).astype(F32)
            sums = jnp.sum(part[:, None] * hot, axis=0)
        copies = jnp.broadcast_to(sums, (groups * reps, sums.shape[0]))
        return lax.all_to_all(copies, ("grp", "rep"), split_axis=0, concat_axis=0, tiled=True)

    def inverse_norm(sums):
        sums = jnp.sum(sums, axis=0)
        if images == 1:
            sums = jnp.repeat(sums, n)[:, None]
        else:
            hot = (image_rows[:, None] == jnp.arange(reps * images)[None, :]).astype(F32)
            sums = jnp.sum(hot * sums[None, :], axis=1, keepdims=True)
        return 1.0 / (sums / (IMG_TOK * width) + 1e-05)

    def cuts_of(count):
        wide = up_weights.shape[2] // count
        return [slice(i * wide, (i + 1) * wide) for i in range(count)]

    first_cuts = cuts_of(FIRST_PARTS if reps == 4 else 1)
    part_count = PARTS if reps == 4 else 1
    cuts = cuts_of(part_count)

    order = Order()
    box = {}

    def until(*keys):
        while not all(key in box for key in keys):
            yield []
        return [box[key] for key in keys]

    def block(model, values, factor, cuts):
        results = yield from staggered(
            [forward(order, values, factor, up_weights[model, :, c], down_weights[model, c]) for c in cuts]
        )
        pres = [pre for pre, _, _ in results]
        return pres, [h for _, h, _ in results], tp_sum(sum(out for _, _, out in results))

    def back_part(name, model, upstream, pre, i, cut):
        yield from delayed(i, iter(()))
        box[name, i] = yield from backward(order, upstream, pre, down_weights[model, cut])

    def block_back(name, model, upstream, pres, cuts):
        return together(
            *[back_part(name, model, upstream, pre, i, cut) for i, (pre, cut) in enumerate(zip(pres, cuts))]
        )

    def swap_rows(student, fake):
        along_y = jnp.where(g >= 2, student, fake)
        return (yield [
            ("grp", ((2, 0), (3, 1), (1, 3)), along_y),
            ("grp", ((2, 3),), fake),
            ("grp", ((0, 3),), fake),
        ])

    def to_student(value):
        (got,) = yield [("grp", ((2, 0), (3, 1)), value)]
        return got

    def to_fake(value):
        return (yield [("grp", ((1, 3),), value), ("grp", ((2, 3),), value), ("grp", ((0, 3),), value)])

    def first_block():
        box["pres_s"], hidden, out = yield from block(0, normed, None, first_cuts)
        box["hidden_s"] = hidden
        made = (x_in.astype(F32) + out).astype(BF16)
        box["made"] = made.astype(F32)
        noised = ((1.0 - sigma) * box["made"] + sigma * renoise.astype(F32)).astype(BF16)
        return made, noised.astype(F32)

    made, noised_f = order.drive(first_block())
    made_f = box["made"]
    scaled = noised_f * cond_part
    is_fake = g == 3
    keep = (g != 2).astype(BF16)

    def token_factor():
        squares = yield from butterfly(jnp.sum(noised_f * noised_f, axis=1), "rep")
        box["factor"] = lax.rsqrt(squares[:, None] / width + 1e-06)

    def factor_ready():
        return (yield from until("factor"))[0]

    def fake_branch():
        values = (scaled * own_gains[2][None, :]).astype(BF16)
        pres, box["hidden_f"], out = yield from block(2, values, factor_ready, cuts)
        box["fake"] = (noised_f + out).astype(BF16).astype(F32)
        box["push_f"] = ((box["fake"] - made_f) * push_scale).astype(BF16)
        yield from block_back("grad_f", 2, box["push_f"], pres, cuts)

    def teacher_branch():
        values = (scaled * own_gains[1][None, :]).astype(BF16)
        _, _, out = yield from block(1, values, factor_ready, cuts)
        box["real"] = (noised_f + out).astype(BF16).astype(F32)

    def student_branch():
        fake, real = yield from until("fake", "real")
        box["raw"] = (fake - real) * push_scale
        box["sums"] = image_sums(order.after(jnp.sum(jnp.abs(made_f - real), axis=1)))
        yield from block_back("grad_s", 0, box["raw"].astype(BF16), box["pres_s"], first_cuts)

    def hidden_moves():
        yield from until("hidden_f", "push_f", "factor", "sums")
        normed_f = (noised_f * box["factor"] * own_gains[2][None, :] * cond_part).astype(BF16)
        box["own_f"] = jnp.concatenate([normed_f, box["push_f"]] + box["hidden_f"], axis=1)
        student = jnp.concatenate(box["hidden_s"], axis=1)
        student = jnp.pad(student, ((0, 0), (2 * own_width, 0)))
        student, _ = lax.optimization_barrier((student, box["sums"]))
        own_f, _ = lax.optimization_barrier((box["own_f"], box["sums"]))
        return (yield from swap_rows(student, own_f))

    def fake_grads(i):
        (value,) = yield from until(("grad_f", i))
        return (yield from to_fake(value))

    def student_grads(i):
        (value,) = yield from until(("grad_s", i))
        return (yield from to_student(value))

    def student_pair():
        yield from until("sums")
        yield from delayed(PAIR_AT, iter(()))
        inverse = inverse_norm(box["sums"])
        scaled_in = (normed.astype(F32) * inverse).astype(BF16)
        box["pair_s"] = jnp.concatenate([scaled_in, (box["raw"] * inverse).astype(BF16)], axis=1)
        box["pair_y"] = yield from to_student(box["pair_s"])

    def generated_out():
        yield from delayed(MADE_AT, iter(()))
        whole = lax.all_to_all(order.after(made), "rep", split_axis=0, concat_axis=1, tiled=True)
        tp_width = noise_in.shape[1]
        mine = lax.dynamic_slice_in_dim(whole, lax.axis_index("tp") * tp_width, tp_width, 1)
        yield []
        others = yield [("grp", [(i, i ^ step) for i in range(groups)], mine) for step in range(1, groups)]
        blocks = jnp.stack([mine] + list(others))
        box["generated"] = jnp.concatenate([jnp.take(blocks, g ^ i, axis=0) for i in (0, 2, 1, 3)], axis=0)

    def second_half():
        return (yield from together(
            fake_branch(),
            delayed(TEACHER_AT, teacher_branch()),
            student_branch(),
            token_factor(),
            hidden_moves(),
            *[fake_grads(i) for i in range(len(cuts))],
            *[student_grads(i) for i in range(len(first_cuts))],
            generated_out(),
            student_pair(),
        ))

    results = order.drive(second_half())[:-2]
    (moved_y, moved_x, moved_d), grads = results[4], results[5:]
    grads_f, grads_s = grads[:part_count], grads[part_count:]
    pair_width = 2 * own_width

    def stacked(student, fake, student_y, fake_3):
        own = jnp.where(is_fake, fake, student)
        from_y = jnp.where(is_fake, fake_3[0], student_y)
        return jnp.concatenate([own, from_y, fake_3[1], fake_3[2]], axis=0)

    moved = (moved_y, moved_x, moved_d)
    pair_all = stacked(
        box["pair_s"] * keep,
        box["own_f"][:, :pair_width] * keep,
        box["pair_y"],
        [m[:, :pair_width] for m in moved],
    )
    normed_all, push_all = pair_all[:, :own_width], pair_all[:, own_width:]
    hidden_all = stacked(
        jnp.concatenate(box["hidden_s"], axis=1),
        box["own_f"][:, pair_width:],
        moved_y[:, pair_width:],
        [m[:, pair_width:] for m in moved],
    )
    grad_s = [box["grad_s", i] for i in range(len(first_cuts))]
    grad_f = [box["grad_f", i] for i in range(len(cuts))]
    grad_all = stacked(
        jnp.concatenate(grad_s, axis=1),
        jnp.concatenate(grad_f, axis=1),
        jnp.concatenate(grads_s, axis=1),
        [jnp.concatenate(list(moved), axis=1) for moved in zip(*grads_f)],
    )

    generated = box["generated"]
    down_grad = dot(hidden_all.T, push_all)
    up_grad = dot(normed_all.T, grad_all)
    return (generated, up_grad[None], down_grad[None])


def solution(mesh):
    in_specs = (
        P("rep", "tp"),
        P("rep", "tp"),
        P("rep", None),
        P("rep"),
        P(),
        P(None, "rep", "tp"),
        P(None, "tp", "rep"),
    )
    out_specs = (P("rep", "tp"), P("grp", "rep", "tp"), P("grp", "tp", "rep"))
    return jax.shard_map(body, mesh=mesh, in_specs=in_specs, out_specs=out_specs, check_vma=False)
```
